32 devices in a mesh: sta: 16 (over z, y, x), tm: 2 (over core).
Axes of the slice: x: 2, y: 2, z: 4, core: 2. Of those that a mesh axis runs over, the one named last changes fastest.
Arguments:
- strain: bfloat16 [24000, 4096], P('tm', 'sta')
- masks: int32 [2], replicated, may hold values from 1 to 15, as said below
- pair_local: int32 [2, 4096], P(None, 'sta'), may hold values from 0 to 255
- pair_remote: int32 [2, 4096], P(None, 'sta'), may hold values from 0 to 255
- owner: int32 [8192, 1], P('sta'), may hold values from 0 to 15; in each aligned block of 512 rows (0 to 511, 512 to 1023, ...) at most 64 rows name the same one
Outputs:
- correlations: float32 [16384, 512], P('sta', 'tm')
The draws below stay inside these ranges and needn't reach their ends.
Inputs may be any that keep to these rules, and one draw needn't show every extreme that they name: `masks`: the 2 entries are distinct, and one of them is 15. At most 64 of the 512 pairs of one station group have the same owner.
All inputs are finite; a program needn't handle non-finite values.
Results may differ from the reference program's by a relative error of at most 0.0051.
Values may be sent and summed in bfloat16 or wider, within the bound.
A program may use at most 64 MiB of HBM per device.

```python
import math
import jax
import jax.numpy as jnp
import numpy as np
from jax import lax

CH_DEV = 256
SEG_LEN = 6000
SEGS_DEV = 2
FREQS = 512
WIN = 32
LAGS = 512
ROUNDS = 2
PAIRS = 256
CAP = 64
CHANNELS = 4096
SAMPLES = 24000
N_STA = 16
N_TM = 2


def draw_strain(key, part):
    keys = jax.random.split(key, 5)
    channel_scale = jnp.exp(jax.random.uniform(keys[0], (CHANNELS,), jnp.float32, 0.0, math.log(10.0)))
    noise = jax.random.normal(keys[1], (SAMPLES, CHANNELS), jnp.float32)
    tone_size = jax.random.uniform(keys[4], (CHANNELS,), jnp.float32, 0.02, 0.2)
    tone_bin = jax.random.randint(keys[2], (CHANNELS,), 1, FREQS + 1, dtype=jnp.int32)
    tone_shift = jax.random.randint(keys[3], (CHANNELS,), 0, SEG_LEN, dtype=jnp.int32)
    sample_index = jnp.arange(SAMPLES, dtype=jnp.int32)[:, None]
    angles = jnp.mod(tone_bin[None, :] * sample_index + tone_shift[None, :], SEG_LEN).astype(jnp.float32) * jnp.float32(2.0 * math.pi / SEG_LEN)
    return (channel_scale[None, :] * (noise + tone_size[None, :] * jnp.cos(angles))).astype(jnp.bfloat16)


def draw_masks(key, part):
    first_key, order_key = jax.random.split(key)
    others = jax.random.permutation(first_key, N_STA - 2)[:ROUNDS - 1] + 1
    full_mask = jnp.full((1,), N_STA - 1, dtype=jnp.int32)
    joined = jnp.concatenate([full_mask, others.astype(jnp.int32)], axis=0)
    return jax.random.permutation(order_key, joined).astype(jnp.int32)


def place_ends(drawn, key, smallest, top_value):
    extent = drawn.shape
    place = [jax.random.randint(jax.random.fold_in(key, axis), (), 0, extent[axis]) for axis in range(len(extent))]
    drawn = drawn.at[tuple(place)].set(smallest)
    longest = extent.index(max(extent))
    place[longest] = (place[longest] + 1) % extent[longest]
    return drawn.at[tuple(place)].set(top_value)


def assign_block(rng, own, number, rows, amount, top, reach, skew):
    ranking = jax.random.permutation(rng, amount)
    heavy_load, ordinary = portions_of(amount, rows * top, reach, skew, True), portions_of(amount, rows * top, reach, skew, False)
    places = jnp.arange(amount)

    def named(sizes, turn):
        used = int((sizes > 0).sum())
        fixed = max(1, used // 4)
        passed = fixed + (places - fixed + turn * (used - fixed)) % max(1, amount - fixed)
        return jnp.zeros((amount,), jnp.int32).at[ranking[jnp.where(places < fixed, places, passed)]].set(jnp.asarray(sizes, jnp.int32))

    sizes = jnp.where(number % 4 == 0, named(heavy_load, number // 4), named(ordinary, number - number // 4 - 1))
    mixed = jax.random.permutation(jax.random.fold_in(own, 3), amount)
    giver, sink = mixed[0:amount // 2 * 2:2], mixed[1:amount // 2 * 2:2]
    margin = jnp.minimum(sizes[giver] - 1, reach - sizes[sink]) // 2
    margin = jnp.where((giver == ranking[0]) | (sink == ranking[0]) | (sizes[sink] == 0), 0, jnp.maximum(margin, 0))
    passed = jax.random.randint(jax.random.fold_in(own, 4), (amount // 2,), 0, 1 << 20) % (margin + 1)
    sizes = sizes.at[giver].add(-passed).at[sink].add(passed)
    members = jnp.searchsorted(jnp.cumsum(sizes), jnp.arange(rows * top), side="right").astype(jnp.int32)
    listing = members.reshape(top, rows).T
    listing = listing[jax.random.permutation(jax.random.fold_in(own, 1), rows)]
    turn = jax.random.randint(jax.random.fold_in(own, 2), (rows, 1), 0, top)
    return jnp.take_along_axis(listing, (jnp.arange(top)[None, :] + turn) % top, axis=1)


def portions_of(amount, total, bound, lean, full):
    loads = [(1 << 20) // math.isqrt(grade ** lean) + 1 for grade in range(1, amount + 1)]
    largest = bound if full else min(bound, max(-(-total // amount), total * loads[0] // sum(loads)))
    least = 1 if total - largest >= amount - 1 else 0
    holding, spare = [largest] + [least] * (amount - 1), total - largest - least * (amount - 1)
    while spare > 0:
        movable = [i for i in range(1, amount) if holding[i] < largest] or [i for i in range(1, amount) if holding[i] < bound]
        whole, left = sum([loads[i] for i in movable]), spare
        for i in movable:
            addition = min(bound - holding[i], max(1, left * loads[i] // whole), spare)
            holding[i] = holding[i] + addition
            spare = spare - addition
    return np.array(holding)


def setup_inputs(seed: int = 0) -> dict:
    key_list = jax.random.split(jax.random.key(seed), 6)
    strain = draw_strain(jax.random.fold_in(key_list[5], 71), 0)
    masks = draw_masks(jax.random.fold_in(key_list[5], 71), 0)
    pair_local = place_ends(jax.random.randint(key_list[2], (ROUNDS, N_STA * PAIRS), 0, CH_DEV), jax.random.fold_in(key_list[2], 1), 0, CH_DEV - 1).astype(jnp.int32)
    pair_remote = place_ends(jax.random.randint(key_list[3], (ROUNDS, N_STA * PAIRS), 0, CH_DEV), jax.random.fold_in(key_list[3], 1), 0, CH_DEV - 1).astype(jnp.int32)
    owner_keys = jax.random.split(jax.random.fold_in(key_list[4], 1), (N_STA * ROUNDS * PAIRS) // (ROUNDS * PAIRS))
    owner_turns = jax.random.permutation(jax.random.fold_in(key_list[4], 3), (N_STA * ROUNDS * PAIRS) // (ROUNDS * PAIRS))
    owner = jax.vmap(lambda own, number: assign_block(jax.random.fold_in(key_list[4], 2), own, number, ROUNDS * PAIRS, N_STA, 1, CAP, 2))(owner_keys, owner_turns).reshape((N_STA * ROUNDS * PAIRS, 1))
    return {"strain": strain, "masks": masks, "pair_local": pair_local, "pair_remote": pair_remote, "owner": owner}


EPSILON = 1e-06

def forward_table():
    freq_bins = (jnp.arange(FREQS, dtype=jnp.int32) + 1)[:, None]
    sample_index = jnp.arange(SEG_LEN, dtype=jnp.int32)[None, :]
    angles = jnp.mod(freq_bins * sample_index, SEG_LEN).astype(jnp.float32) * jnp.float32(2.0 * math.pi / SEG_LEN)
    return jnp.concatenate([jnp.cos(angles), -jnp.sin(angles)], axis=0).astype(jnp.bfloat16)

def inverse_table(first_lag, lag_count):
    freq_bins = (jnp.arange(FREQS, dtype=jnp.int32) + 1)[:, None]
    lag_index = first_lag + jnp.arange(lag_count, dtype=jnp.int32)[None, :] - LAGS // 2
    angles = jnp.mod(freq_bins * lag_index, SEG_LEN).astype(jnp.float32) * jnp.float32(2.0 * math.pi / SEG_LEN)
    return jnp.concatenate([jnp.cos(angles), -jnp.sin(angles)], axis=0)

def band_table():
    row_index = jnp.arange(FREQS, dtype=jnp.int32)[:, None]
    col_index = jnp.arange(FREQS, dtype=jnp.int32)[None, :]
    within = jnp.abs(row_index - col_index) <= WIN
    return jnp.where(within, jnp.float32(1.0 / (2 * WIN + 1)), jnp.float32(0.0))

def whiten(spectra):
    real_part = spectra[:, :FREQS]
    imag_part = spectra[:, FREQS:]
    amplitude = jnp.sqrt(real_part * real_part + imag_part * imag_part)
    smoothed = jnp.einsum('jk,sjc->skc', band_table(), amplitude, precision=lax.Precision.HIGHEST)
    divisor = jnp.concatenate([smoothed, smoothed], axis=1) + EPSILON
    return (spectra / divisor).astype(jnp.bfloat16)

def cross_rows(own_block, peer_block, local_index, remote_index):
    own_rows = jnp.take(own_block, local_index, axis=2).astype(jnp.float32)
    peer_rows = jnp.take(peer_block, remote_index, axis=2).astype(jnp.float32)
    own_real, own_imag = (own_rows[:, :FREQS], own_rows[:, FREQS:])
    peer_real, peer_imag = (peer_rows[:, :FREQS], peer_rows[:, FREQS:])
    real_sum = lax.optimization_barrier(jnp.sum(own_real * peer_real + own_imag * peer_imag, axis=0))
    imag_sum = lax.optimization_barrier(jnp.sum(own_imag * peer_real - own_real * peer_imag, axis=0))
    return jnp.concatenate([real_sum, imag_sum], axis=0).T

def slots_of(owners, slot_count):
    one_hot = (owners[:, None] == jnp.arange(slot_count, dtype=jnp.int32)[None, :]).astype(jnp.int32)
    earlier = jnp.cumsum(one_hot, axis=0) - one_hot
    return lax.optimization_barrier(jnp.sum(earlier * one_hot, axis=1)).astype(jnp.int32)

def reference(strain, masks, pair_local, pair_remote, owner):
    forward = forward_table().astype(jnp.float32)
    seg_total = SEGS_DEV * N_TM

    def group_spectra(group):
        block = lax.dynamic_slice_in_dim(strain, (group * CH_DEV).astype(jnp.int32), CH_DEV, axis=1).astype(jnp.float32)
        segments = block.reshape(seg_total, SEG_LEN, CH_DEV)
        spectra = jnp.einsum('kl,slc->skc', forward, segments, precision=lax.Precision.HIGHEST)
        return whiten(spectra)
    whitened_all = lax.map(group_spectra, jnp.arange(N_STA, dtype=jnp.int32))
    inverse = inverse_table(jnp.int32(0), LAGS)
    norm_scale = 1.0 / math.sqrt(seg_total * FREQS)

    def group_rows(group):
        rows_list = []
        for round_index in range(ROUNDS):
            partner = jnp.bitwise_xor(group, masks[round_index]).astype(jnp.int32)
            local_index = lax.dynamic_slice_in_dim(pair_local[round_index], (group * PAIRS).astype(jnp.int32), PAIRS)
            remote_index = lax.dynamic_slice_in_dim(pair_remote[round_index], (group * PAIRS).astype(jnp.int32), PAIRS)
            rows_list.append(cross_rows(whitened_all[group], whitened_all[partner], local_index, remote_index))
        pair_rows = jnp.concatenate(rows_list, axis=0)
        lagged = jnp.dot(pair_rows, inverse, precision=lax.Precision.HIGHEST) * norm_scale
        owners = lax.dynamic_slice_in_dim(owner[:, 0], (group * ROUNDS * PAIRS).astype(jnp.int32), ROUNDS * PAIRS)
        targets = owners * (N_STA * CAP) + group * CAP + slots_of(owners, N_STA)
        return (lagged, targets.astype(jnp.int32))
    lagged_all, targets_all = lax.map(group_rows, jnp.arange(N_STA, dtype=jnp.int32))
    result = jnp.zeros((N_STA * N_STA * CAP, LAGS), jnp.float32)
    return result.at[targets_all.reshape(-1)].set(lagged_all.reshape(-1, LAGS))
```

```python
import math

import jax
import jax.numpy as jnp
import ml_dtypes
import numpy as np
from jax import lax
from jax.sharding import PartitionSpec as P

SEG_LEN = 6000
FREQS = 512
WIN = 32
LAGS = 512
EPSILON = 1e-06
BF16 = jnp.bfloat16


def angles_of(product):
    return np.mod(product, SEG_LEN).astype(np.float32) * np.float32(2.0 * math.pi / SEG_LEN)


def forward_table():
    angles = angles_of(np.arange(1, FREQS + 1)[:, None] * np.arange(SEG_LEN)[None, :])
    return np.concatenate([np.cos(angles), -np.sin(angles)], axis=0).astype(ml_dtypes.bfloat16)


def inverse_table():
    angles = angles_of(np.arange(1, FREQS + 1)[:, None] * (np.arange(LAGS) - LAGS // 2)[None, :])
    return np.concatenate([np.cos(angles), -np.sin(angles)], axis=0).astype(ml_dtypes.bfloat16)


def band_table():
    row = np.arange(FREQS)
    return (np.abs(row[:, None] - row[None, :]) <= WIN).astype(ml_dtypes.bfloat16)


def matmul(spec, left, right):
    return jnp.einsum(spec, left, right, preferred_element_type=jnp.float32)


def whiten(spectra):
    real_part = spectra[:, :FREQS]
    imag_part = spectra[:, FREQS:]
    amplitude = jnp.sqrt(real_part * real_part + imag_part * imag_part)
    high = amplitude.astype(BF16)
    low = (amplitude - high.astype(jnp.float32)).astype(BF16)
    band = jnp.asarray(band_table())
    total = matmul("kj,sjc->skc", band, high) + matmul("kj,sjc->skc", band, low)
    inverse = 1.0 / (total * (1.0 / (2 * WIN + 1)) + EPSILON)
    return (spectra * jnp.concatenate([inverse, inverse], axis=1)).astype(BF16)


def exchange_with(mask, group_count):
    def run(*arrays):
        pairs = [(i, i ^ mask) for i in range(group_count)]
        return tuple(lax.ppermute(a, "sta", pairs) for a in arrays)

    return run


def swap(other, group_count, full_arrays, other_arrays):
    def branch(mask):
        def run(full_in, other_in):
            return (
                exchange_with(group_count - 1, group_count)(*full_in),
                exchange_with(mask, group_count)(*other_in),
            )

        return run

    branches = [branch(mask) for mask in range(1, group_count - 1)]
    return lax.switch(other - 1, branches, full_arrays, other_arrays)


def one_hot(index, count):
    return (index[None, :] == jnp.arange(count, dtype=jnp.int32)[:, None]).astype(BF16)


def cross_of(kept, arrived, kept_index, arrived_index, sign):
    channels = kept.shape[1]
    mine = matmul("kc,cp->kp", kept, one_hot(kept_index, channels))
    theirs = matmul("kc,cp->kp", arrived, one_hot(arrived_index, channels))
    ar, ai, br, bi = mine[:FREQS], mine[FREQS:], theirs[:FREQS], theirs[FREQS:]
    return jnp.concatenate([ar * br + ai * bi, (ai * br - ar * bi) * sign], axis=0).astype(BF16)


def targets_of(owners, group_count, capacity):
    hot = (owners[:, None] == jnp.arange(group_count, dtype=jnp.int32)[None, :]).astype(jnp.float32)
    rows = np.arange(owners.shape[0])
    before = (rows[None, :] < rows[:, None]).astype(ml_dtypes.bfloat16)
    earlier = matmul("ij,jo->io", jnp.asarray(before), hot.astype(BF16))
    return owners * capacity + jnp.sum(earlier * hot, axis=1).astype(jnp.int32)


def per_device(strain, masks, pair_local, pair_remote, owner):
    group_count = lax.axis_size("sta")
    time_count = lax.axis_size("tm")
    seg_count = strain.shape[0] // SEG_LEN
    channels = strain.shape[1]
    round_count, pair_count = pair_local.shape
    capacity = max(2, 2 * round_count * pair_count // group_count)
    full_mask = group_count - 1
    other = masks[0] + masks[1] - full_mask
    full_first = masks[0] == full_mask

    def by_mask(array):
        return jnp.where(full_first, array, array[::-1])

    local_index, remote_index = by_mask(pair_local), by_mask(pair_remote)
    targets = targets_of(owner[:, 0], group_count, capacity)
    targets = by_mask(targets.reshape(round_count, pair_count)).reshape(-1)

    segments = strain.reshape(seg_count, SEG_LEN, channels)
    spectra = matmul("kl,slc->skc", jnp.asarray(forward_table()), segments)
    whitened = whiten(spectra)

    upper = jnp.bitwise_and(lax.axis_index("sta"), jnp.bitwise_and(other, -other)) != 0
    sent = jnp.where(upper, whitened[1], whitened[0])
    kept = jnp.where(upper, whitened[0], whitened[1])

    index = jnp.stack([local_index, remote_index], axis=1)
    arrived = swap(other, group_count, (sent, index[0]), (sent, index[1]))
    sign = np.concatenate([np.ones(pair_count), -np.ones(pair_count)]).astype(np.float32)[None, :]
    crosses = []
    for number, (peer, peer_index) in enumerate(arrived):
        kept_index = jnp.concatenate([local_index[number], peer_index[1]])
        arrived_index = jnp.concatenate([remote_index[number], peer_index[0]])
        crosses.append(cross_of(kept, peer, kept_index, arrived_index, sign))
    cross = jnp.concatenate(crosses, axis=1)
    norm_scale = 1.0 / math.sqrt(seg_count * time_count * FREQS)
    lagged = matmul("kp,kl->pl", cross, jnp.asarray(inverse_table())) * norm_scale

    width = LAGS // time_count
    first_half = lax.axis_index("tm") == 0
    halves = lagged[:, :width], lagged[:, width:]
    mine = jnp.where(first_half, halves[0], halves[1])
    theirs = jnp.where(first_half, halves[1], halves[0]).astype(BF16)
    lags = mine + lax.ppermute(theirs, "tm", [(0, 1), (1, 0)]).astype(jnp.float32)

    lags = lags.reshape(round_count, 2, pair_count, width)
    back = lags[:, 1].astype(BF16)
    returned = swap(other, group_count, (back[0],), (back[1],))
    total = lags[:, 0] + jnp.stack([r[0] for r in returned]).astype(jnp.float32)
    rows = total.reshape(round_count * pair_count, width).astype(BF16)
    outgoing = matmul("ps,pl->sl", one_hot(targets, group_count * capacity).T, rows).astype(BF16)
    received = lax.all_to_all(outgoing, "sta", split_axis=0, concat_axis=0, tiled=True)
    return received.astype(jnp.float32)


def solution(mesh):
    placed = (P("tm", "sta"), P(), P(None, "sta"), P(None, "sta"), P("sta", None))
    return jax.shard_map(
        per_device, mesh=mesh, in_specs=placed, out_specs=P("sta", "tm"), check_vma=False
    )
```

```python
import math

import jax
import jax.numpy as jnp
import ml_dtypes
import numpy as np
from jax import lax
from jax.experimental import pallas as pl
from jax.experimental.pallas import tpu as pltpu
from jax.sharding import PartitionSpec as P

SEG_LEN = 6000
FREQS = 512
WIN = 32
LAGS = 512
EPSILON = 1e-06
BF16 = jnp.bfloat16


def angles_of(product):
    return np.mod(product, SEG_LEN).astype(np.float32) * np.float32(2.0 * math.pi / SEG_LEN)


def forward_table():
    angles = angles_of(np.arange(1, FREQS + 1)[:, None] * np.arange(SEG_LEN)[None, :])
    return np.concatenate([np.cos(angles), -np.sin(angles)], axis=0).astype(ml_dtypes.bfloat16)


def inverse_table():
    angles = angles_of(np.arange(1, FREQS + 1)[:, None] * (np.arange(LAGS) - LAGS // 2)[None, :])
    return np.concatenate([np.cos(angles), -np.sin(angles)], axis=0).astype(ml_dtypes.bfloat16)


def band_table():
    row = np.arange(FREQS)
    return (np.abs(row[:, None] - row[None, :]) <= WIN).astype(ml_dtypes.bfloat16)


def matmul(spec, left, right):
    return jnp.einsum(spec, left, right, preferred_element_type=jnp.float32)


def whiten(spectra):
    real_part = spectra[:, :FREQS]
    imag_part = spectra[:, FREQS:]
    amplitude = jnp.sqrt(real_part * real_part + imag_part * imag_part)
    high = amplitude.astype(BF16)
    low = (amplitude - high.astype(jnp.float32)).astype(BF16)
    band = jnp.asarray(band_table())
    total = matmul("kj,sjc->skc", band, high) + matmul("kj,sjc->skc", band, low)
    inverse = 1.0 / (total * (1.0 / (2 * WIN + 1)) + EPSILON)
    return (spectra * jnp.concatenate([inverse, inverse], axis=1)).astype(BF16)


def exchange_with(mask, group_count, arrays):
    pairs = [(i, i ^ mask) for i in range(group_count)]
    return tuple(lax.ppermute(a, "sta", pairs) for a in arrays)


def swap_other(other, group_count, arrays):
    def branch(mask):
        return lambda *given: exchange_with(mask, group_count, given)

    branches = [branch(mask) for mask in range(1, group_count - 1)]
    return lax.switch(other - 1, branches, *arrays)


def to_owners(outgoing, group_count, capacity):
    width = outgoing.shape[1]

    def kernel(out_ref, in_ref, own_sem, send_sems, recv_sems):
        me = lax.axis_index("sta")
        barrier = pltpu.get_barrier_semaphore()
        for step in range(1, group_count):
            pl.semaphore_signal(
                barrier,
                inc=1,
                device_id={"sta": (me + step) % group_count},
                device_id_type=pl.DeviceIdType.MESH,
            )
        mine = pl.ds(pl.multiple_of(me * capacity, capacity), capacity)
        own = pltpu.make_async_copy(out_ref.at[mine], in_ref.at[mine], own_sem)
        own.start()
        pl.semaphore_wait(barrier, group_count - 1)
        copies = []
        for step in range(1, group_count):
            target = (me + step) % group_count
            rows = pl.ds(pl.multiple_of(target * capacity, capacity), capacity)
            copy = pltpu.make_async_remote_copy(
                src_ref=out_ref.at[rows],
                dst_ref=in_ref.at[mine],
                send_sem=send_sems.at[step - 1],
                recv_sem=recv_sems.at[step - 1],
                device_id={"sta": target},
                device_id_type=pl.DeviceIdType.MESH,
            )
            copy.start()
            copies.append(copy)
        own.wait()
        for copy in copies:
            copy.wait()

    return pl.pallas_call(
        kernel,
        out_shape=jax.ShapeDtypeStruct((group_count * capacity, width), BF16),
        in_specs=[pl.BlockSpec(memory_space=pltpu.VMEM)],
        out_specs=pl.BlockSpec(memory_space=pltpu.VMEM),
        scratch_shapes=[
            pltpu.SemaphoreType.DMA(()),
            pltpu.SemaphoreType.DMA((group_count - 1,)),
            pltpu.SemaphoreType.DMA((group_count - 1,)),
        ],
        compiler_params=pltpu.CompilerParams(collective_id=0, has_side_effects=True),
    )(outgoing)


def one_hot(index, count):
    return (index[None, :] == jnp.arange(count, dtype=jnp.int32)[:, None]).astype(BF16)


def cross_of(kept, arrived, kept_index, arrived_index, sign):
    channels = kept.shape[1]
    mine = matmul("kc,cp->kp", kept, one_hot(kept_index, channels))
    theirs = matmul("kc,cp->kp", arrived, one_hot(arrived_index, channels))
    ar, ai, br, bi = mine[:FREQS], mine[FREQS:], theirs[:FREQS], theirs[FREQS:]
    return jnp.concatenate([ar * br + ai * bi, (ai * br - ar * bi) * sign], axis=0).astype(BF16)


def targets_of(owners, group_count, capacity):
    hot = (owners[:, None] == jnp.arange(group_count, dtype=jnp.int32)[None, :]).astype(jnp.float32)
    rows = np.arange(owners.shape[0])
    before = (rows[None, :] < rows[:, None]).astype(ml_dtypes.bfloat16)
    earlier = matmul("ij,jo->io", jnp.asarray(before), hot.astype(BF16))
    return owners * capacity + jnp.sum(earlier * hot, axis=1).astype(jnp.int32)


def per_device(strain, masks, pair_local, pair_remote, owner):
    group_count = lax.axis_size("sta")
    time_count = lax.axis_size("tm")
    seg_count = strain.shape[0] // SEG_LEN
    channels = strain.shape[1]
    round_count, pair_count = pair_local.shape
    capacity = max(2, 2 * round_count * pair_count // group_count)
    full_mask = group_count - 1
    other = masks[0] + masks[1] - full_mask
    full_first = masks[0] == full_mask

    def by_mask(array):
        return jnp.where(full_first, array[0], array[1]), jnp.where(full_first, array[1], array[0])

    targets = targets_of(owner[:, 0], group_count, capacity)
    targets = jnp.concatenate(by_mask(targets.reshape(round_count, pair_count)))
    local_index, remote_index = by_mask(pair_local), by_mask(pair_remote)
    index = [jnp.stack(pair) for pair in zip(local_index, remote_index)]

    upper = jnp.bitwise_and(lax.axis_index("sta"), jnp.bitwise_and(other, -other)) != 0
    upper = upper.astype(jnp.int32)
    segments = strain.reshape(seg_count, SEG_LEN, channels)
    table = jnp.asarray(forward_table())

    def whitened_of(number):
        segment = lax.dynamic_slice_in_dim(segments, number, 1, axis=0)
        return whiten(matmul("kl,slc->skc", table, segment))[0]

    sent = whitened_of(upper)
    full_peer = exchange_with(group_count - 1, group_count, (index[0], sent))
    other_peer = swap_other(other, group_count, (sent, index[1]))
    kept_number, other_sent, other_index = lax.optimization_barrier((1 - upper, *other_peer))
    kept = whitened_of(kept_number)

    sign = np.concatenate([np.ones(pair_count), -np.ones(pair_count)]).astype(np.float32)[None, :]
    inverse = jnp.asarray(inverse_table())
    norm_scale = 1.0 / math.sqrt(seg_count * time_count * FREQS)
    width = LAGS // time_count
    first_half = lax.axis_index("tm") == 0

    def lags_of(number, peer, peer_index):
        kept_index = jnp.concatenate([local_index[number], peer_index[1]])
        arrived_index = jnp.concatenate([remote_index[number], peer_index[0]])
        cross = cross_of(kept, peer, kept_index, arrived_index, sign)
        lagged = matmul("kp,kl->pl", cross, inverse) * norm_scale
        halves = lagged[:, :width], lagged[:, width:]
        mine = jnp.where(first_half, halves[0], halves[1])
        theirs = jnp.where(first_half, halves[1], halves[0]).astype(BF16)
        return mine + lax.ppermute(theirs, "tm", [(0, 1), (1, 0)]).astype(jnp.float32)

    other_lags = lags_of(1, other_sent, other_index)
    full_lags = lags_of(0, full_peer[1], full_peer[0])
    [full_back] = exchange_with(group_count - 1, group_count, (full_lags[pair_count:].astype(BF16),))
    [other_back] = swap_other(other, group_count, (other_lags[pair_count:].astype(BF16),))
    full_total = full_lags[:pair_count] + full_back.astype(jnp.float32)
    other_total = other_lags[:pair_count] + other_back.astype(jnp.float32)
    rows = jnp.concatenate([full_total, other_total]).astype(BF16)
    outgoing = matmul("ps,pl->sl", one_hot(targets, group_count * capacity).T, rows).astype(BF16)
    return to_owners(outgoing, group_count, capacity).astype(jnp.float32)


def solution(mesh):
    placed = (P("tm", "sta"), P(), P(None, "sta"), P(None, "sta"), P("sta", None))
    return jax.shard_map(
        per_device, mesh=mesh, in_specs=placed, out_specs=P("sta", "tm"), check_vma=False
    )
```

```python
import math

import jax
import jax.numpy as jnp
import ml_dtypes
import numpy as np
from jax import lax
from jax.experimental import pallas as pl
from jax.experimental.pallas import tpu as pltpu
from jax.sharding import PartitionSpec as P

SEG_LEN = 6000
FREQS = 512
WIN = 32
LAGS = 512
EPSILON = 1e-06
BF16 = jnp.bfloat16


def angles_of(product):
    return np.mod(product, SEG_LEN).astype(np.float32) * np.float32(2.0 * math.pi / SEG_LEN)


def forward_table():
    angles = angles_of(np.arange(1, FREQS + 1)[:, None] * np.arange(SEG_LEN)[None, :])
    return np.concatenate([np.cos(angles), -np.sin(angles)], axis=0).astype(ml_dtypes.bfloat16)


def inverse_table():
    angles = angles_of(np.arange(1, FREQS + 1)[:, None] * (np.arange(LAGS) - LAGS // 2)[None, :])
    return np.concatenate([np.cos(angles), -np.sin(angles)], axis=0).astype(ml_dtypes.bfloat16)


def band_table():
    row = np.arange(FREQS)
    return (np.abs(row[:, None] - row[None, :]) <= WIN).astype(ml_dtypes.bfloat16)


def matmul(spec, left, right):
    return jnp.einsum(spec, left, right, preferred_element_type=jnp.float32)


def whiten(spectra):
    real_part = spectra[:, :FREQS]
    imag_part = spectra[:, FREQS:]
    amplitude = jnp.sqrt(real_part * real_part + imag_part * imag_part)
    high = amplitude.astype(BF16)
    low = (amplitude - high.astype(jnp.float32)).astype(BF16)
    band = jnp.asarray(band_table())
    total = matmul("kj,sjc->skc", band, high) + matmul("kj,sjc->skc", band, low)
    inverse = 1.0 / (total * (1.0 / (2 * WIN + 1)) + EPSILON)
    return (spectra * jnp.concatenate([inverse, inverse], axis=1)).astype(BF16)


def exchange_with(mask, group_count, arrays):
    pairs = [(i, i ^ mask) for i in range(group_count)]
    return tuple(lax.ppermute(a, "sta", pairs) for a in arrays)


def switched(other, group_count, run, *arrays):
    branches = [
        lambda *given, mask=mask: run(mask, *given) for mask in range(1, group_count - 1)
    ]
    return lax.switch(other - 1, branches, *arrays)


def to_owners(outgoing, group_count, capacity):
    width = outgoing.shape[1]

    def kernel(out_ref, in_ref, own_sem, send_sems, recv_sems):
        me = lax.axis_index("sta")
        barrier = pltpu.get_barrier_semaphore()
        for step in range(1, group_count):
            pl.semaphore_signal(
                barrier,
                inc=1,
                device_id={"sta": (me + step) % group_count},
                device_id_type=pl.DeviceIdType.MESH,
            )
        mine = pl.ds(pl.multiple_of(me * capacity, capacity), capacity)
        own = pltpu.make_async_copy(out_ref.at[mine], in_ref.at[mine], own_sem)
        own.start()
        pl.semaphore_wait(barrier, group_count - 1)
        copies = []
        for step in range(1, group_count):
            target = (me + step) % group_count
            rows = pl.ds(pl.multiple_of(target * capacity, capacity), capacity)
            copy = pltpu.make_async_remote_copy(
                src_ref=out_ref.at[rows],
                dst_ref=in_ref.at[mine],
                send_sem=send_sems.at[step - 1],
                recv_sem=recv_sems.at[step - 1],
                device_id={"sta": target},
                device_id_type=pl.DeviceIdType.MESH,
            )
            copy.start()
            copies.append(copy)
        own.wait()
        for copy in copies:
            copy.wait()

    return pl.pallas_call(
        kernel,
        out_shape=jax.ShapeDtypeStruct((group_count * capacity, width), BF16),
        in_specs=[pl.BlockSpec(memory_space=pltpu.VMEM)],
        out_specs=pl.BlockSpec(memory_space=pltpu.VMEM),
        scratch_shapes=[
            pltpu.SemaphoreType.DMA(()),
            pltpu.SemaphoreType.DMA((group_count - 1,)),
            pltpu.SemaphoreType.DMA((group_count - 1,)),
        ],
        compiler_params=pltpu.CompilerParams(collective_id=0, has_side_effects=True),
    )(outgoing)


def one_hot(index, count):
    return (index[None, :] == jnp.arange(count, dtype=jnp.int32)[:, None]).astype(BF16)


def cross_of(kept, arrived, kept_index, arrived_index, sign):
    channels = kept.shape[1]
    mine = matmul("kc,cp->kp", kept, one_hot(kept_index, channels))
    theirs = matmul("kc,cp->kp", arrived, one_hot(arrived_index, channels))
    ar, ai, br, bi = mine[:FREQS], mine[FREQS:], theirs[:FREQS], theirs[FREQS:]
    return jnp.concatenate([ar * br + ai * bi, (ai * br - ar * bi) * sign], axis=0).astype(BF16)


def targets_of(owners, group_count, capacity):
    hot = (owners[:, None] == jnp.arange(group_count, dtype=jnp.int32)[None, :]).astype(jnp.float32)
    rows = np.arange(owners.shape[0])
    before = (rows[None, :] < rows[:, None]).astype(ml_dtypes.bfloat16)
    earlier = matmul("ij,jo->io", jnp.asarray(before), hot.astype(BF16))
    return owners * capacity + jnp.sum(earlier * hot, axis=1).astype(jnp.int32)


def per_device(strain, masks, pair_local, pair_remote, owner):
    group_count = lax.axis_size("sta")
    time_count = lax.axis_size("tm")
    seg_count = strain.shape[0] // SEG_LEN
    channels = strain.shape[1]
    round_count, pair_count = pair_local.shape
    capacity = max(2, 2 * round_count * pair_count // group_count)
    full_mask = group_count - 1
    other = masks[0] + masks[1] - full_mask
    full_first = masks[0] == full_mask

    def by_mask(array):
        return jnp.where(full_first, array[0], array[1]), jnp.where(full_first, array[1], array[0])

    targets = targets_of(owner[:, 0], group_count, capacity)
    targets = jnp.concatenate(by_mask(targets.reshape(round_count, pair_count)))
    local_index, remote_index = by_mask(pair_local), by_mask(pair_remote)
    index = [jnp.stack(pair) for pair in zip(local_index, remote_index)]

    upper = jnp.bitwise_and(lax.axis_index("sta"), jnp.bitwise_and(other, -other)) != 0
    upper = upper.astype(jnp.int32)
    segments = strain.reshape(seg_count, SEG_LEN, channels)
    table = jnp.asarray(forward_table())

    def whitened_of(number):
        segment = lax.dynamic_slice_in_dim(segments, number, 1, axis=0)
        return whiten(matmul("kl,slc->skc", table, segment))[0]

    index_rows = jnp.concatenate(index, axis=0).astype(BF16)
    index_rows = jnp.pad(index_rows, ((0, 16 - 2 * round_count), (0, 0)))
    sent = jnp.concatenate([whitened_of(upper), index_rows], axis=0)
    [full_peer] = exchange_with(group_count - 1, group_count, (sent,))
    kept = whitened_of(1 - upper)
    sent, kept = lax.optimization_barrier((sent, kept))
    [other_peer] = switched(
        other, group_count, lambda mask, a: exchange_with(mask, group_count, (a,)), sent
    )

    sign = np.concatenate([np.ones(pair_count), -np.ones(pair_count)]).astype(np.float32)[None, :]
    inverse = jnp.asarray(inverse_table())
    norm_scale = 1.0 / math.sqrt(seg_count * time_count * FREQS)
    width = LAGS // time_count
    first_half = lax.axis_index("tm") == 0

    def lags_of(number, arrived):
        peer = arrived[: 2 * FREQS]
        first = 2 * FREQS + 2 * number
        peer_index = arrived[first : first + 2].astype(jnp.int32)
        kept_index = jnp.concatenate([local_index[number], peer_index[1]])
        arrived_index = jnp.concatenate([remote_index[number], peer_index[0]])
        cross = cross_of(kept, peer, kept_index, arrived_index, sign)
        lagged = matmul("kp,kl->pl", cross, inverse) * norm_scale
        halves = lagged[:, :width], lagged[:, width:]
        mine = jnp.where(first_half, halves[0], halves[1])
        theirs = jnp.where(first_half, halves[1], halves[0]).astype(BF16)
        return mine + lax.ppermute(theirs, "tm", [(0, 1), (1, 0)]).astype(jnp.float32)

    other_lags = lags_of(1, other_peer)
    full_lags = lags_of(0, full_peer)
    full_back, other_back = switched(
        other,
        group_count,
        lambda mask, a, b: (
            *exchange_with(group_count - 1, group_count, (a,)),
            *exchange_with(mask, group_count, (b,)),
        ),
        full_lags[pair_count:].astype(BF16),
        other_lags[pair_count:].astype(BF16),
    )
    full_total = full_lags[:pair_count] + full_back.astype(jnp.float32)
    other_total = other_lags[:pair_count] + other_back.astype(jnp.float32)
    rows = jnp.concatenate([full_total, other_total]).astype(BF16)
    outgoing = matmul("ps,pl->sl", one_hot(targets, group_count * capacity).T, rows).astype(BF16)
    return to_owners(outgoing, group_count, capacity).astype(jnp.float32)


def solution(mesh):
    placed = (P("tm", "sta"), P(), P(None, "sta"), P(None, "sta"), P("sta", None))
    return jax.shard_map(
        per_device, mesh=mesh, in_specs=placed, out_specs=P("sta", "tm"), check_vma=False
    )
```

```python
import math

import jax
import jax.numpy as jnp
import ml_dtypes
import numpy as np
from jax import lax
from jax.experimental import pallas as pl
from jax.experimental.pallas import tpu as pltpu
from jax.sharding import PartitionSpec as P

SEG_LEN = 6000
FREQS = 512
WIN = 32
LAGS = 512
EPSILON = 1e-06
BF16 = jnp.bfloat16


def angles_of(product):
    return np.mod(product, SEG_LEN).astype(np.float32) * np.float32(2.0 * math.pi / SEG_LEN)


def forward_table():
    angles = angles_of(np.arange(1, FREQS + 1)[:, None] * np.arange(SEG_LEN)[None, :])
    return np.concatenate([np.cos(angles), -np.sin(angles)], axis=0).astype(ml_dtypes.bfloat16)


def inverse_table():
    angles = angles_of(np.arange(1, FREQS + 1)[:, None] * (np.arange(LAGS) - LAGS // 2)[None, :])
    return np.concatenate([np.cos(angles), -np.sin(angles)], axis=0).astype(ml_dtypes.bfloat16)


def band_table():
    row = np.arange(FREQS)
    return (np.abs(row[:, None] - row[None, :]) <= WIN).astype(ml_dtypes.bfloat16)


def matmul(spec, left, right):
    return jnp.einsum(spec, left, right, preferred_element_type=jnp.float32)


def whiten(spectra):
    real_part = spectra[:, :FREQS]
    imag_part = spectra[:, FREQS:]
    amplitude = jnp.sqrt(real_part * real_part + imag_part * imag_part)
    high = amplitude.astype(BF16)
    low = (amplitude - high.astype(jnp.float32)).astype(BF16)
    band = jnp.asarray(band_table())
    total = matmul("kj,sjc->skc", band, high) + matmul("kj,sjc->skc", band, low)
    inverse = 1.0 / (total * (1.0 / (2 * WIN + 1)) + EPSILON)
    return (spectra * jnp.concatenate([inverse, inverse], axis=1)).astype(BF16)


def exchange_with(mask, group_count, arrays):
    pairs = [(i, i ^ mask) for i in range(group_count)]
    return tuple(lax.ppermute(a, "sta", pairs) for a in arrays)


def switched(other, group_count, run, *arrays):
    branches = [
        lambda *given, mask=mask: run(mask, *given) for mask in range(1, group_count - 1)
    ]
    return lax.switch(other - 1, branches, *arrays)


def to_owners(outgoing, group_count, capacity):
    width = outgoing.shape[1]

    def kernel(out_ref, in_ref, own_sem, send_sems, recv_sems):
        me = lax.axis_index("sta")
        barrier = pltpu.get_barrier_semaphore()
        for step in range(1, group_count):
            pl.semaphore_signal(
                barrier,
                inc=1,
                device_id={"sta": (me + step) % group_count},
                device_id_type=pl.DeviceIdType.MESH,
            )
        mine = pl.ds(pl.multiple_of(me * capacity, capacity), capacity)
        own = pltpu.make_async_copy(out_ref.at[mine], in_ref.at[mine], own_sem)
        own.start()
        pl.semaphore_wait(barrier, group_count - 1)
        copies = []
        for step in range(1, group_count):
            target = (me + step) % group_count
            rows = pl.ds(pl.multiple_of(target * capacity, capacity), capacity)
            copy = pltpu.make_async_remote_copy(
                src_ref=out_ref.at[rows],
                dst_ref=in_ref.at[mine],
                send_sem=send_sems.at[step - 1],
                recv_sem=recv_sems.at[step - 1],
                device_id={"sta": target},
                device_id_type=pl.DeviceIdType.MESH,
            )
            copy.start()
            copies.append(copy)
        own.wait()
        for copy in copies:
            copy.wait()

    return pl.pallas_call(
        kernel,
        out_shape=jax.ShapeDtypeStruct((group_count * capacity, width), BF16),
        in_specs=[pl.BlockSpec(memory_space=pl.ANY)],
        out_specs=pl.BlockSpec(memory_space=pl.ANY),
        scratch_shapes=[
            pltpu.SemaphoreType.DMA(()),
            pltpu.SemaphoreType.DMA((group_count - 1,)),
            pltpu.SemaphoreType.DMA((group_count - 1,)),
        ],
        compiler_params=pltpu.CompilerParams(collective_id=0, has_side_effects=True),
    )(outgoing)


def one_hot(index, count):
    return (index[None, :] == jnp.arange(count, dtype=jnp.int32)[:, None]).astype(BF16)


def cross_of(kept, arrived, kept_index, arrived_index, sign):
    channels = kept.shape[1]
    mine = matmul("kc,cp->kp", kept, one_hot(kept_index, channels))
    theirs = matmul("kc,cp->kp", arrived, one_hot(arrived_index, channels))
    ar, ai, br, bi = mine[:FREQS], mine[FREQS:], theirs[:FREQS], theirs[FREQS:]
    return jnp.concatenate([ar * br + ai * bi, (ai * br - ar * bi) * sign], axis=0).astype(BF16)


def targets_of(owners, group_count, capacity):
    hot = (owners[:, None] == jnp.arange(group_count, dtype=jnp.int32)[None, :]).astype(jnp.float32)
    rows = np.arange(owners.shape[0])
    before = (rows[None, :] < rows[:, None]).astype(ml_dtypes.bfloat16)
    earlier = matmul("ij,jo->io", jnp.asarray(before), hot.astype(BF16))
    return owners * capacity + jnp.sum(earlier * hot, axis=1).astype(jnp.int32)


def per_device(strain, masks, pair_local, pair_remote, owner):
    group_count = lax.axis_size("sta")
    time_count = lax.axis_size("tm")
    seg_count = strain.shape[0] // SEG_LEN
    channels = strain.shape[1]
    round_count, pair_count = pair_local.shape
    capacity = max(2, 2 * round_count * pair_count // group_count)
    full_mask = group_count - 1
    other = masks[0] + masks[1] - full_mask
    full_first = masks[0] == full_mask

    def by_mask(array):
        return jnp.where(full_first, array[0], array[1]), jnp.where(full_first, array[1], array[0])

    targets = targets_of(owner[:, 0], group_count, capacity)
    targets = jnp.concatenate(by_mask(targets.reshape(round_count, pair_count)))
    local_index, remote_index = by_mask(pair_local), by_mask(pair_remote)
    index = [jnp.stack(pair) for pair in zip(local_index, remote_index)]

    upper = jnp.bitwise_and(lax.axis_index("sta"), jnp.bitwise_and(other, -other)) != 0
    upper = upper.astype(jnp.int32)
    segments = strain.reshape(seg_count, SEG_LEN, channels)
    table = jnp.asarray(forward_table())

    def whitened_of(number):
        segment = lax.dynamic_slice_in_dim(segments, number, 1, axis=0)
        return whiten(matmul("kl,slc->skc", table, segment))[0]

    index_rows = jnp.concatenate(index, axis=0).astype(BF16)
    index_rows = jnp.pad(index_rows, ((0, 16 - 2 * round_count), (0, 0)))
    sent = jnp.concatenate([whitened_of(upper), index_rows], axis=0)
    [full_peer] = exchange_with(group_count - 1, group_count, (sent,))
    kept = whitened_of(1 - upper)
    sent, kept = lax.optimization_barrier((sent, kept))
    [other_peer] = switched(
        other, group_count, lambda mask, a: exchange_with(mask, group_count, (a,)), sent
    )

    sign = np.concatenate([np.ones(pair_count), -np.ones(pair_count)]).astype(np.float32)[None, :]
    inverse = jnp.asarray(inverse_table())
    norm_scale = 1.0 / math.sqrt(seg_count * time_count * FREQS)
    width = LAGS // time_count
    first_half = lax.axis_index("tm") == 0

    def lags_of(number, arrived):
        peer = arrived[: 2 * FREQS]
        first = 2 * FREQS + 2 * number
        peer_index = arrived[first : first + 2].astype(jnp.int32)
        kept_index = jnp.concatenate([local_index[number], peer_index[1]])
        arrived_index = jnp.concatenate([remote_index[number], peer_index[0]])
        cross = cross_of(kept, peer, kept_index, arrived_index, sign)
        lagged = matmul("kp,kl->pl", cross, inverse) * norm_scale
        halves = lagged[:, :width], lagged[:, width:]
        mine = jnp.where(first_half, halves[0], halves[1])
        theirs = jnp.where(first_half, halves[1], halves[0]).astype(BF16)
        return mine + lax.ppermute(theirs, "tm", [(0, 1), (1, 0)]).astype(jnp.float32)

    other_lags = lags_of(1, other_peer)
    full_lags = lags_of(0, full_peer)
    full_back, other_back = switched(
        other,
        group_count,
        lambda mask, a, b: (
            *exchange_with(group_count - 1, group_count, (a,)),
            *exchange_with(mask, group_count, (b,)),
        ),
        full_lags[pair_count:].astype(BF16),
        other_lags[pair_count:].astype(BF16),
    )
    full_total = full_lags[:pair_count] + full_back.astype(jnp.float32)
    other_total = other_lags[:pair_count] + other_back.astype(jnp.float32)
    rows = jnp.concatenate([full_total, other_total]).astype(BF16)
    outgoing = matmul("ps,pl->sl", one_hot(targets, group_count * capacity).T, rows).astype(BF16)
    return to_owners(outgoing, group_count, capacity).astype(jnp.float32)


def solution(mesh):
    placed = (P("tm", "sta"), P(), P(None, "sta"), P(None, "sta"), P("sta", None))
    return jax.shard_map(
        per_device, mesh=mesh, in_specs=placed, out_specs=P("sta", "tm"), check_vma=False
    )
```
